32 devices in a mesh: blk: 4 (over y, x), mode: 8 (over z, core).
Axes of the slice: x: 2, y: 2, z: 4, core: 2. Of those that a mesh axis runs over, the one named last changes fastest.
Arguments:
- density: bfloat16 [2, 128, 1024, 256], P(None, 'mode', 'blk'), may hold values from -6 to 6
- kernel_tiles: bfloat16 [128, 8, 4, 2, 128, 128], P('mode', 'blk'), may hold values from -0.1875 to 0.1875
- tile_index: int32 [128, 8, 4], P('mode', 'blk'), may hold values from 0 to 1
- coupling: bfloat16 [2, 9, 128, 1024], P(None, None, 'mode', 'blk'), may hold values from -4 to 4
- spread: int32 [1024], P('blk'), may hold values from 0 to 4
- liner: int32 [1024], P('blk'), may hold values 0 or 1
Outputs:
- applied: bfloat16 [2, 128, 1024, 256], P(None, 'mode', 'blk')
The draws below stay inside these ranges and needn't reach their ends.
Inputs may be any that keep to these rules, and one draw needn't show every extreme that they name: `tile_index`: each retained tile names one column tile of its source shard.
All inputs are finite; a program needn't handle non-finite values. No bound on the sum of `liner` on one device may be relied on, other than what follows from the above.
Results may differ from the reference program's by a relative error of at most 0.0033.
Values may be sent and summed in bfloat16 or wider, within the bound.
A program may use at most 320 MiB of HBM per device.

```python
import jax
import jax.numpy as jnp
from jax import lax

MODES = 128
PDEV = 256
POINTS = 1024
TILE = 128
ROWT = 8
RHS = 256
BWMAX = 4
BAND = 9
N_BLK = 4


def plant(drawn, rng, low, top_value):
    shape = drawn.shape
    spot = [jax.random.randint(jax.random.fold_in(rng, axis), (), 0, shape[axis]) for axis in range(len(shape))]
    drawn = drawn.at[tuple(spot)].set(low)
    longest = shape.index(max(shape))
    spot[longest] = (spot[longest] + 1) % shape[longest]
    return drawn.at[tuple(spot)].set(top_value)


def shard_levels(stream_key, extent, cuts, smallest, top_value):
    factor_of = 1.0
    for axis_at, blocks in cuts:
        steps = jax.random.uniform(jax.random.fold_in(jax.random.fold_in(stream_key, 6), axis_at), (blocks,), jnp.float32, smallest / len(cuts), top_value / len(cuts))
        factor_of = factor_of * jnp.repeat(jnp.exp(steps), extent[axis_at] // blocks).reshape((-1,) + (1,) * (len(extent) - 1 - axis_at))
    return factor_of


def gaussian(stream_key, extent, scale, most, pieces=(), held_as=jnp.bfloat16):
    level = shard_levels(stream_key, extent, pieces, -0.22, 0.18) if pieces else 1.0
    result = jax.random.normal(stream_key, extent, jnp.float32) * scale * level
    return jnp.minimum(jnp.maximum(result, -most), most).astype(held_as)


def setup_inputs(seed: int = 0) -> dict:
    keys = jax.random.split(jax.random.key(seed), 7)
    density = gaussian(keys[0], (2, MODES, POINTS, RHS), 1.0, 6.0, ((1, 8), (2, 4)))
    kernel_tiles = gaussian(keys[1], (MODES, ROWT, N_BLK, 2, TILE, TILE), (2 * TILE * N_BLK) ** -0.5, 0.1875, ((0, 8), (1, 4)))
    tile_index = plant(jax.random.randint(keys[2], (MODES, ROWT, N_BLK), 0, PDEV // TILE), jax.random.fold_in(keys[2], 1), 0, (PDEV // TILE) - 1).astype(jnp.int32)
    coupling = gaussian(keys[3], (2, BAND, MODES, POINTS), 0.4, 4.0, ((2, 8), (3, 4)))
    spread = plant(jax.random.randint(keys[4], (POINTS,), 0, BWMAX + 1), jax.random.fold_in(keys[4], 1), 0, BWMAX).astype(jnp.int32)
    liner = plant((jax.random.randint(keys[5], (POINTS,), 0, 3) < 1).astype(jnp.int32), jax.random.fold_in(keys[5], 1), 0, 1)
    return {"density": density, "kernel_tiles": kernel_tiles, "tile_index": tile_index, "coupling": coupling, "spread": spread, "liner": liner}


def reference(density, kernel_tiles, tile_index, coupling, spread, liner):
    per_shard = PDEV // TILE
    column_tiles = (jnp.arange(N_BLK, dtype=jnp.int32) * per_shard)[None, None, :] + tile_index
    by_mode = jnp.transpose(density.reshape(2, MODES, POINTS // TILE, TILE, RHS), (1, 0, 2, 3, 4))

    def one_mode(inputs):
        kernel_mode, column_mode, sigma_mode = inputs
        picked = sigma_mode[:, column_mode].astype(jnp.float32)
        kernel_float = kernel_mode.astype(jnp.float32)
        real_part = jnp.einsum("tbqk,tbkr->tqr", kernel_float[:, :, 0], picked[0]) - jnp.einsum("tbqk,tbkr->tqr", kernel_float[:, :, 1], picked[1])
        imag_part = jnp.einsum("tbqk,tbkr->tqr", kernel_float[:, :, 0], picked[1]) + jnp.einsum("tbqk,tbkr->tqr", kernel_float[:, :, 1], picked[0])
        return jnp.stack([real_part, imag_part])

    near_modes = lax.map(one_mode, (kernel_tiles, column_tiles, by_mode))
    near = jnp.transpose(near_modes, (1, 0, 2, 3, 4)).reshape(2, MODES, POINTS, RHS)

    offsets = jnp.abs(jnp.arange(BAND, dtype=jnp.int32) - BWMAX)
    within = (offsets[:, None] <= spread[None, :]) & (liner[None, :] == 1)
    weights = coupling * within[None, :, None, :].astype(jnp.bfloat16)
    padded = jnp.pad(density, ((0, 0), (BWMAX, BWMAX), (0, 0), (0, 0)))
    real_part = jnp.zeros((MODES, POINTS, RHS), jnp.float32)
    imag_part = jnp.zeros((MODES, POINTS, RHS), jnp.float32)
    for offset in range(BAND):
        shifted = padded[:, offset:offset + MODES].astype(jnp.float32)
        weight_now = weights[:, offset].astype(jnp.float32)[..., None]
        real_part = real_part + weight_now[0] * shifted[0] - weight_now[1] * shifted[1]
        imag_part = imag_part + weight_now[0] * shifted[1] + weight_now[1] * shifted[0]
    coupled = jnp.stack([real_part, imag_part]).astype(jnp.bfloat16)
    total = 0.5 * density.astype(jnp.float32) + near + coupled.astype(jnp.float32)
    return total.astype(jnp.bfloat16)
```

```python
import functools

import jax
import jax.numpy as jnp
from jax import lax
from jax.experimental import pallas as pl
from jax.experimental.pallas import tpu as pltpu
from jax.sharding import PartitionSpec as P

F32 = jnp.float32
BF16 = jnp.bfloat16
MIB = 1024 * 1024
ROWS = 32


def operator_kernel(
    cfg, index_ref, spread_ref, liner_ref, coupling_ref, density_ref, tiles_ref, out_ref,
    extended, gathered, tiles, result, coupling32, raw, weights,
    own_sems, forward_sems, arrive_sems, halo_send, halo_arrive, local_sems, out_sems,
):
    shards, groups, step, modes, reach, mode_devices = cfg
    high_count = shards // 2
    band = 2 * reach + 1
    row_tiles = tiles_ref.shape[1]
    tile = tiles_ref.shape[-1]
    points = density_ref.shape[2]
    blk = lax.axis_index("blk")
    mode_at = lax.axis_index("mode")
    high, low = blk // 2, blk % 2
    partner = high * 2 + (1 - low)

    def along(k):
        return lax.rem(high + k, high_count) * 2 + low

    def part(g):
        return pl.ds(g * step, step)

    def own_copy(c, k, g):
        target = partner if k == 0 else along(k)
        slot = 0 if k == 0 else (high_count - k) * 2 - 1
        return pltpu.make_async_remote_copy(
            src_ref=density_ref.at[c, part(g)],
            dst_ref=gathered.at[slot, c, part(g)],
            send_sem=own_sems.at[c, k, g],
            recv_sem=arrive_sems.at[slot, c, g],
            device_id={"blk": target},
        )

    def forward_copy(c, k, g):
        if c == 0:
            source, slot, target = 0, (high_count - k) * 2, along(k)
        else:
            source, slot, target = k * 2 - 1, k * 2, partner
        return pltpu.make_async_remote_copy(
            src_ref=gathered.at[source, c, part(g)],
            dst_ref=gathered.at[slot, c, part(g)],
            send_sem=forward_sems.at[c, k - 1, g],
            recv_sem=arrive_sems.at[slot, c, g],
            device_id={"blk": target},
        )

    def arrived(slot, c, g):
        pltpu.make_async_remote_copy(
            src_ref=gathered.at[slot, c, part(g)],
            dst_ref=gathered.at[slot, c, part(g)],
            send_sem=arrive_sems.at[slot, c, g],
            recv_sem=arrive_sems.at[slot, c, g],
            device_id={"blk": partner},
        ).wait_recv()

    def halo_copy(side):
        source = modes - reach if side == 0 else 0
        target = reach + modes if side == 1 else 0
        neighbour = mode_at + 1 if side == 0 else mode_at - 1
        return pltpu.make_async_remote_copy(
            src_ref=density_ref.at[:, pl.ds(source, reach)],
            dst_ref=extended.at[:, pl.ds(target, reach)],
            send_sem=halo_send.at[side],
            recv_sem=halo_arrive.at[side],
            device_id={"mode": neighbour},
        )

    has_left = mode_at > 0
    has_right = mode_at < mode_devices - 1

    own_load = pltpu.make_async_copy(
        density_ref, extended.at[:, pl.ds(reach, modes)], local_sems.at[0]
    )
    tiles_load = pltpu.make_async_copy(tiles_ref, tiles, local_sems.at[1])
    own_load.start()
    tiles_load.start()

    barrier = pltpu.get_barrier_semaphore()
    pl.semaphore_signal(barrier, inc=1, device_id={"blk": partner})
    for k in range(1, high_count):
        pl.semaphore_signal(barrier, inc=1, device_id={"blk": along(k)})

    @pl.when(has_left)
    def _():
        pl.semaphore_signal(barrier, inc=1, device_id={"mode": mode_at - 1})

    @pl.when(has_right)
    def _():
        pl.semaphore_signal(barrier, inc=1, device_id={"mode": mode_at + 1})

    peers = high_count + jnp.where(has_left, 1, 0) + jnp.where(has_right, 1, 0)
    pl.semaphore_wait(barrier, peers)

    @pl.when(has_right)
    def _():
        halo_copy(0).start()

    @pl.when(has_left)
    def _():
        halo_copy(1).start()

    @pl.loop(0, groups)
    def _(g):
        own_copy(0, 0, g).start()
        for k in range(1, high_count):
            own_copy(1, k, g).start()

    @pl.loop(0, groups)
    def _(g):
        own_copy(1, 0, g).start()
        for k in range(1, high_count):
            own_copy(0, k, g).start()

    coupling32[...] = coupling_ref[...].astype(F32)
    raw[...] = jnp.zeros_like(raw)

    @pl.when(jnp.logical_not(has_left))
    def _():
        extended[:, pl.ds(0, reach)] = jnp.zeros((2, reach) + extended.shape[2:], BF16)

    @pl.when(jnp.logical_not(has_right))
    def _():
        extended[:, pl.ds(reach + modes, reach)] = jnp.zeros((2, reach) + extended.shape[2:], BF16)

    own_load.wait()

    @pl.when(has_left)
    def _():
        halo_copy(0).wait_recv()

    @pl.when(has_right)
    def _():
        halo_copy(1).wait_recv()

    def couple_mode(m):
        on_liner = liner_ref[...] == 1
        reach_of = spread_ref[...]
        for d in range(band):
            inside = jnp.where(on_liner & (reach_of >= abs(d - reach)), 1.0, 0.0).astype(F32)
            for c in range(2):
                raw[pl.ds(c * band + d, 1), :] = coupling32[c, d, pl.ds(m, 1), :] * inside
        weights[...] = jnp.transpose(raw[...])

        @pl.loop(0, points // ROWS)
        def _(b):
            rows = pl.ds(pl.multiple_of(b * ROWS, ROWS), ROWS)
            weight = weights[rows, :]
            real = jnp.zeros((ROWS, extended.shape[3]), F32)
            imag = jnp.zeros((ROWS, extended.shape[3]), F32)
            for d in range(band):
                shifted_r = extended[0, m + d, rows, :].astype(F32)
                shifted_i = extended[1, m + d, rows, :].astype(F32)
                w_r = weight[:, d : d + 1]
                w_i = weight[:, band + d : band + d + 1]
                real = real + w_r * shifted_r - w_i * shifted_i
                imag = imag + w_r * shifted_i + w_i * shifted_r
            result[0, m, rows, :] = real.astype(BF16)
            result[1, m, rows, :] = imag.astype(BF16)

    @pl.loop(0, groups)
    def _(g):
        arrived(0, 0, g)
        for k in range(1, high_count):
            forward_copy(0, k, g).start()
        for k in range(1, high_count):
            arrived(k * 2 - 1, 1, g)
            forward_copy(1, k, g).start()

        @pl.loop(0, step)
        def _(j):
            couple_mode(g * step + j)

    tiles_load.wait()

    def near_mode(m):
        for r in range(row_tiles):
            total = None
            for slot in range(-1, shards - 1):
                dk, dl = (slot + 1) // 2, (slot + 1) % 2
                source = lax.rem(high + dk, high_count) * 2 + (low if dl == 0 else 1 - low)
                which = index_ref[m, r, source]
                picked = []
                for c in range(2):
                    if slot < 0:
                        block = extended[c, reach + m]
                    else:
                        block = gathered[slot, c, m]
                    chosen = block[:tile]
                    for t in range(1, points // tile):
                        chosen = lax.select(which == t, block[t * tile : (t + 1) * tile], chosen)
                    picked.append(chosen)
                k_r = tiles[m, r, source, 0]
                k_i = tiles[m, r, source, 1]
                left = jnp.concatenate(
                    [jnp.concatenate([k_r, -k_i], axis=1), jnp.concatenate([k_i, k_r], axis=1)], axis=0
                )
                product = jnp.dot(left, jnp.concatenate(picked, axis=0), preferred_element_type=F32)
                total = product if total is None else total + product
            rows = pl.ds(r * tile, tile)
            for c in range(2):
                value = 0.5 * extended[c, reach + m, rows, :].astype(F32)
                value = value + total[c * tile : (c + 1) * tile] + result[c, m, rows, :].astype(F32)
                result[c, m, rows, :] = value.astype(BF16)

    def out_copy(g):
        return pltpu.make_async_copy(result.at[:, part(g)], out_ref.at[:, part(g)], out_sems.at[g])

    @pl.loop(0, groups)
    def _(g):
        arrived(0, 1, g)
        for k in range(1, high_count):
            arrived(k * 2 - 1, 0, g)
            arrived(k * 2, 0, g)
            arrived(k * 2, 1, g)

        @pl.loop(0, step)
        def _(j):
            near_mode(g * step + j)

        out_copy(g).start()

    @pl.loop(0, groups)
    def _(g):
        for c in range(2):
            for k in range(high_count):
                own_copy(c, k, g).wait_send()
            for k in range(1, high_count):
                forward_copy(c, k, g).wait_send()
        out_copy(g).wait()

    @pl.when(has_right)
    def _():
        halo_copy(0).wait_send()

    @pl.when(has_left)
    def _():
        halo_copy(1).wait_send()


def apply_local(mode_devices, shard_count, density, kernel_tiles, tile_index, coupling, spread, liner):
    modes, points, rhs = density.shape[1:]
    band = coupling.shape[1]
    reach = band // 2
    groups = 8 if modes % 8 == 0 else modes
    step = modes // groups
    high_count = shard_count // 2
    dma = pltpu.SemaphoreType.DMA
    vmem = pl.BlockSpec(memory_space=pltpu.VMEM)
    cfg = (shard_count, groups, step, modes, reach, mode_devices)
    return pl.pallas_call(
        functools.partial(operator_kernel, cfg),
        out_shape=jax.ShapeDtypeStruct(density.shape, BF16),
        in_specs=[
            pl.BlockSpec(memory_space=pltpu.SMEM), vmem, vmem, vmem,
            pl.BlockSpec(memory_space=pl.ANY), pl.BlockSpec(memory_space=pl.ANY),
        ],
        out_specs=pl.BlockSpec(memory_space=pl.ANY),
        scratch_shapes=[
            pltpu.VMEM((2, modes + 2 * reach, points, rhs), BF16),
            pltpu.VMEM((shard_count - 1, 2, modes, points, rhs), BF16),
            pltpu.VMEM(kernel_tiles.shape, BF16),
            pltpu.VMEM(density.shape, BF16),
            pltpu.VMEM(coupling.shape, F32),
            pltpu.VMEM((128, points), F32),
            pltpu.VMEM((points, 128), F32),
            dma((2, high_count, groups)),
            dma((2, max(high_count - 1, 1), groups)),
            dma((shard_count - 1, 2, groups)),
            dma((2,)),
            dma((2,)),
            dma((2,)),
            dma((groups,)),
        ],
        compiler_params=pltpu.CompilerParams(
            collective_id=0, has_side_effects=True, vmem_limit_bytes=60 * MIB
        ),
    )(tile_index, spread.reshape(1, -1), liner.reshape(1, -1), coupling, density, kernel_tiles)


def solution(mesh):
    body = functools.partial(apply_local, mesh.shape["mode"], mesh.shape["blk"])
    return jax.shard_map(
        body,
        mesh=mesh,
        in_specs=(
            P(None, "mode", "blk", None),
            P("mode", "blk", None, None, None, None),
            P("mode", "blk", None),
            P(None, None, "mode", "blk"),
            P("blk"),
            P("blk"),
        ),
        out_specs=P(None, "mode", "blk", None),
        check_vma=False,
    )
```

```python
import functools

import jax
import jax.numpy as jnp
from jax import lax
from jax.experimental import pallas as pl
from jax.experimental.pallas import tpu as pltpu
from jax.sharding import PartitionSpec as P

F32 = jnp.float32
BF16 = jnp.bfloat16
MIB = 1024 * 1024
ROWS = 32


def operator_kernel(
    cfg, index_ref, spread_ref, liner_ref, coupling_ref, density_ref, tiles_ref, result,
    extended, gathered, tiles, coupling32, raw, weights,
    own_sems, forward_sems, arrive_sems, halo_send, halo_arrive, local_sems,
):
    shards, groups, step, modes, reach, mode_devices = cfg
    high_count = shards // 2
    band = 2 * reach + 1
    row_tiles = tiles_ref.shape[1]
    tile = tiles_ref.shape[-1]
    points = density_ref.shape[2]
    blk = lax.axis_index("blk")
    mode_at = lax.axis_index("mode")
    high, low = blk // 2, blk % 2
    partner = high * 2 + (1 - low)

    def along(k):
        return lax.rem(high + k, high_count) * 2 + low

    def part(g):
        return pl.ds(g * step, step)

    def own_copy(c, k, g):
        target = partner if k == 0 else along(k)
        slot = 0 if k == 0 else (high_count - k) * 2 - 1
        return pltpu.make_async_remote_copy(
            src_ref=density_ref.at[c, part(g)],
            dst_ref=gathered.at[slot, c, part(g)],
            send_sem=own_sems.at[c, k, g],
            recv_sem=arrive_sems.at[slot, c, g],
            device_id={"blk": target},
        )

    def forward_copy(c, k, g):
        if c == 0:
            source, slot, target = 0, (high_count - k) * 2, along(k)
        else:
            source, slot, target = k * 2 - 1, k * 2, partner
        return pltpu.make_async_remote_copy(
            src_ref=gathered.at[source, c, part(g)],
            dst_ref=gathered.at[slot, c, part(g)],
            send_sem=forward_sems.at[c, k - 1, g],
            recv_sem=arrive_sems.at[slot, c, g],
            device_id={"blk": target},
        )

    def arrived(slot, c, g):
        pltpu.make_async_remote_copy(
            src_ref=gathered.at[slot, c, part(g)],
            dst_ref=gathered.at[slot, c, part(g)],
            send_sem=arrive_sems.at[slot, c, g],
            recv_sem=arrive_sems.at[slot, c, g],
            device_id={"blk": partner},
        ).wait_recv()

    def halo_copy(side):
        source = modes - reach if side == 0 else 0
        target = reach + modes if side == 1 else 0
        neighbour = mode_at + 1 if side == 0 else mode_at - 1
        return pltpu.make_async_remote_copy(
            src_ref=density_ref.at[:, pl.ds(source, reach)],
            dst_ref=extended.at[:, pl.ds(target, reach)],
            send_sem=halo_send.at[side],
            recv_sem=halo_arrive.at[side],
            device_id={"mode": neighbour},
        )

    has_left = mode_at > 0
    has_right = mode_at < mode_devices - 1

    own_load = pltpu.make_async_copy(
        density_ref, extended.at[:, pl.ds(reach, modes)], local_sems.at[0]
    )
    tiles_load = pltpu.make_async_copy(tiles_ref, tiles, local_sems.at[1])
    own_load.start()
    tiles_load.start()

    barrier = pltpu.get_barrier_semaphore()
    pl.semaphore_signal(barrier, inc=1, device_id={"blk": partner})
    for k in range(1, high_count):
        pl.semaphore_signal(barrier, inc=1, device_id={"blk": along(k)})

    @pl.when(has_left)
    def _():
        pl.semaphore_signal(barrier, inc=1, device_id={"mode": mode_at - 1})

    @pl.when(has_right)
    def _():
        pl.semaphore_signal(barrier, inc=1, device_id={"mode": mode_at + 1})

    peers = high_count + jnp.where(has_left, 1, 0) + jnp.where(has_right, 1, 0)
    pl.semaphore_wait(barrier, peers)

    @pl.when(has_right)
    def _():
        halo_copy(0).start()

    @pl.when(has_left)
    def _():
        halo_copy(1).start()

    @pl.loop(0, groups)
    def _(g):
        own_copy(0, 0, g).start()
        for k in range(1, high_count):
            own_copy(1, k, g).start()

    @pl.loop(0, groups)
    def _(g):
        own_copy(1, 0, g).start()
        for k in range(1, high_count):
            own_copy(0, k, g).start()

    coupling32[...] = coupling_ref[...].astype(F32)
    raw[...] = jnp.zeros_like(raw)

    @pl.when(jnp.logical_not(has_left))
    def _():
        extended[:, pl.ds(0, reach)] = jnp.zeros((2, reach) + extended.shape[2:], BF16)

    @pl.when(jnp.logical_not(has_right))
    def _():
        extended[:, pl.ds(reach + modes, reach)] = jnp.zeros((2, reach) + extended.shape[2:], BF16)

    own_load.wait()

    @pl.when(has_left)
    def _():
        halo_copy(0).wait_recv()

    @pl.when(has_right)
    def _():
        halo_copy(1).wait_recv()

    def couple_mode(m):
        on_liner = liner_ref[...] == 1
        reach_of = spread_ref[...]
        for d in range(band):
            inside = jnp.where(on_liner & (reach_of >= abs(d - reach)), 1.0, 0.0).astype(F32)
            for c in range(2):
                raw[pl.ds(c * band + d, 1), :] = coupling32[c, d, pl.ds(m, 1), :] * inside
        weights[...] = jnp.transpose(raw[...])

        @pl.loop(0, points // ROWS)
        def _(b):
            rows = pl.ds(pl.multiple_of(b * ROWS, ROWS), ROWS)
            weight = weights[rows, :]
            real = jnp.zeros((ROWS, extended.shape[3]), F32)
            imag = jnp.zeros((ROWS, extended.shape[3]), F32)
            for d in range(band):
                shifted_r = extended[0, m + d, rows, :].astype(F32)
                shifted_i = extended[1, m + d, rows, :].astype(F32)
                w_r = weight[:, d : d + 1]
                w_i = weight[:, band + d : band + d + 1]
                real = real + w_r * shifted_r - w_i * shifted_i
                imag = imag + w_r * shifted_i + w_i * shifted_r
            result[0, m, rows, :] = real.astype(BF16)
            result[1, m, rows, :] = imag.astype(BF16)

    @pl.loop(0, groups)
    def _(g):
        arrived(0, 0, g)
        for k in range(1, high_count):
            forward_copy(0, k, g).start()
        for k in range(1, high_count):
            arrived(k * 2 - 1, 1, g)
            forward_copy(1, k, g).start()

        @pl.loop(0, step)
        def _(j):
            couple_mode(g * step + j)

    tiles_load.wait()

    def near_mode(m):
        for r in range(row_tiles):
            total = None
            for slot in range(-1, shards - 1):
                dk, dl = (slot + 1) // 2, (slot + 1) % 2
                source = lax.rem(high + dk, high_count) * 2 + (low if dl == 0 else 1 - low)
                which = index_ref[r, source, m]
                picked = []
                for c in range(2):
                    if slot < 0:
                        block = extended[c, reach + m]
                    else:
                        block = gathered[slot, c, m]
                    chosen = block[:tile]
                    for t in range(1, points // tile):
                        chosen = lax.select(which == t, block[t * tile : (t + 1) * tile], chosen)
                    picked.append(chosen)
                k_r = tiles[m, r, source, 0]
                k_i = tiles[m, r, source, 1]
                left = jnp.concatenate(
                    [jnp.concatenate([k_r, -k_i], axis=1), jnp.concatenate([k_i, k_r], axis=1)], axis=0
                )
                product = jnp.dot(left, jnp.concatenate(picked, axis=0), preferred_element_type=F32)
                total = product if total is None else total + product
            rows = pl.ds(r * tile, tile)
            for c in range(2):
                value = 0.5 * extended[c, reach + m, rows, :].astype(F32)
                value = value + total[c * tile : (c + 1) * tile] + result[c, m, rows, :].astype(F32)
                result[c, m, rows, :] = value.astype(BF16)

    @pl.loop(0, groups)
    def _(g):
        arrived(0, 1, g)
        for k in range(1, high_count):
            arrived(k * 2 - 1, 0, g)
            arrived(k * 2, 0, g)
            arrived(k * 2, 1, g)

        @pl.loop(0, step)
        def _(j):
            near_mode(g * step + j)

    @pl.loop(0, groups)
    def _(g):
        for c in range(2):
            for k in range(high_count):
                own_copy(c, k, g).wait_send()
            for k in range(1, high_count):
                forward_copy(c, k, g).wait_send()

    @pl.when(has_right)
    def _():
        halo_copy(0).wait_send()

    @pl.when(has_left)
    def _():
        halo_copy(1).wait_send()


def apply_local(mode_devices, shard_count, density, kernel_tiles, tile_index, coupling, spread, liner):
    modes, points, rhs = density.shape[1:]
    band = coupling.shape[1]
    reach = band // 2
    groups = 8 if modes % 8 == 0 else modes
    step = modes // groups
    high_count = shard_count // 2
    dma = pltpu.SemaphoreType.DMA
    vmem = pl.BlockSpec(memory_space=pltpu.VMEM)
    cfg = (shard_count, groups, step, modes, reach, mode_devices)
    return pl.pallas_call(
        functools.partial(operator_kernel, cfg),
        out_shape=pltpu.VMEM(density.shape, BF16),
        in_specs=[
            pl.BlockSpec(memory_space=pltpu.SMEM), vmem, vmem, vmem,
            pl.BlockSpec(memory_space=pltpu.HBM), pl.BlockSpec(memory_space=pltpu.HBM),
        ],
        out_specs=vmem,
        scratch_shapes=[
            pltpu.VMEM((2, modes + 2 * reach, points, rhs), BF16),
            pltpu.VMEM((shard_count - 1, 2, modes, points, rhs), BF16),
            pltpu.VMEM(kernel_tiles.shape, BF16),
            pltpu.VMEM(coupling.shape, F32),
            pltpu.VMEM((128, points), F32),
            pltpu.VMEM((points, 128), F32),
            dma((2, high_count, groups)),
            dma((2, max(high_count - 1, 1), groups)),
            dma((shard_count - 1, 2, groups)),
            dma((2,)),
            dma((2,)),
            dma((2,)),
        ],
        compiler_params=pltpu.CompilerParams(
            collective_id=0, has_side_effects=True, vmem_limit_bytes=56 * MIB
        ),
    )(tile_index.transpose(1, 2, 0), spread.reshape(1, -1), liner.reshape(1, -1), coupling, density, kernel_tiles)


def solution(mesh):
    body = functools.partial(apply_local, mesh.shape["mode"], mesh.shape["blk"])
    return jax.shard_map(
        body,
        mesh=mesh,
        in_specs=(
            P(None, "mode", "blk", None),
            P("mode", "blk", None, None, None, None),
            P("mode", "blk", None),
            P(None, None, "mode", "blk"),
            P("blk"),
            P("blk"),
        ),
        out_specs=P(None, "mode", "blk", None),
        check_vma=False,
    )
```

```python
import functools

import jax
import jax.numpy as jnp
from jax import lax
from jax.experimental import pallas as pl
from jax.experimental.pallas import tpu as pltpu
from jax.sharding import PartitionSpec as P

F32 = jnp.float32
BF16 = jnp.bfloat16
MIB = 1024 * 1024
ROWS = 32


def operator_kernel(
    cfg, index_hbm, spread_ref, liner_ref, coupling_ref, density_ref, tiles_ref, result,
    extended, gathered, tiles, coupling16, spread32, liner32, index_ref, coupling32, raw, weights,
    own_sems, forward_sems, arrive_sems, halo_send, halo_arrive, local_sems,
):
    shards, groups, step, modes, reach, mode_devices = cfg
    high_count = shards // 2
    band = 2 * reach + 1
    row_tiles = tiles_ref.shape[1]
    tile = tiles_ref.shape[-1]
    points = density_ref.shape[2]
    blk = lax.axis_index("blk")
    mode_at = lax.axis_index("mode")
    high, low = blk // 2, blk % 2
    partner = high * 2 + (1 - low)

    def along(k):
        return lax.rem(high + k, high_count) * 2 + low

    def part(g):
        return pl.ds(g * step, step)

    def own_copy(c, k, g):
        target = partner if k == 0 else along(k)
        slot = 0 if k == 0 else (high_count - k) * 2 - 1
        return pltpu.make_async_remote_copy(
            src_ref=density_ref.at[c, part(g)],
            dst_ref=gathered.at[slot, c, part(g)],
            send_sem=own_sems.at[c, k, g],
            recv_sem=arrive_sems.at[slot, c, g],
            device_id={"blk": target},
        )

    def forward_copy(c, k, g):
        if c == 0:
            source, slot, target = 0, (high_count - k) * 2, along(k)
        else:
            source, slot, target = k * 2 - 1, k * 2, partner
        return pltpu.make_async_remote_copy(
            src_ref=gathered.at[source, c, part(g)],
            dst_ref=gathered.at[slot, c, part(g)],
            send_sem=forward_sems.at[c, k - 1, g],
            recv_sem=arrive_sems.at[slot, c, g],
            device_id={"blk": target},
        )

    def arrived(slot, c, g):
        pltpu.make_async_remote_copy(
            src_ref=gathered.at[slot, c, part(g)],
            dst_ref=gathered.at[slot, c, part(g)],
            send_sem=arrive_sems.at[slot, c, g],
            recv_sem=arrive_sems.at[slot, c, g],
            device_id={"blk": partner},
        ).wait_recv()

    def halo_copy(side):
        source = modes - reach if side == 0 else 0
        target = reach + modes if side == 1 else 0
        neighbour = mode_at + 1 if side == 0 else mode_at - 1
        return pltpu.make_async_remote_copy(
            src_ref=density_ref.at[:, pl.ds(source, reach)],
            dst_ref=extended.at[:, pl.ds(target, reach)],
            send_sem=halo_send.at[side],
            recv_sem=halo_arrive.at[side],
            device_id={"mode": neighbour},
        )

    has_left = mode_at > 0
    has_right = mode_at < mode_devices - 1

    own_load = pltpu.make_async_copy(
        density_ref, extended.at[:, pl.ds(reach, modes)], local_sems.at[0]
    )
    tiles_load = pltpu.make_async_copy(tiles_ref, tiles, local_sems.at[1])
    barrier = pltpu.get_barrier_semaphore()
    pl.semaphore_signal(barrier, inc=1, device_id={"blk": partner})
    for k in range(1, high_count):
        pl.semaphore_signal(barrier, inc=1, device_id={"blk": along(k)})

    @pl.when(has_left)
    def _():
        pl.semaphore_signal(barrier, inc=1, device_id={"mode": mode_at - 1})

    @pl.when(has_right)
    def _():
        pl.semaphore_signal(barrier, inc=1, device_id={"mode": mode_at + 1})

    peers = high_count + jnp.where(has_left, 1, 0) + jnp.where(has_right, 1, 0)
    pl.semaphore_wait(barrier, peers)

    @pl.when(has_right)
    def _():
        halo_copy(0).start()

    @pl.when(has_left)
    def _():
        halo_copy(1).start()

    small_loads = [
        pltpu.make_async_copy(source, target, local_sems.at[2 + at])
        for at, (source, target) in enumerate(
            [(coupling_ref, coupling16), (spread_ref, spread32), (liner_ref, liner32), (index_hbm, index_ref)]
        )
    ]
    @pl.loop(0, groups)
    def _(g):
        own_copy(0, 0, g).start()
        for k in range(1, high_count):
            own_copy(1, k, g).start()

    @pl.loop(0, groups)
    def _(g):
        own_copy(1, 0, g).start()
        for k in range(1, high_count):
            own_copy(0, k, g).start()

    for load in small_loads:
        load.start()
    own_load.start()
    tiles_load.start()
    for load in small_loads:
        load.wait()
    coupling32[...] = coupling16[...].astype(F32)
    raw[...] = jnp.zeros_like(raw)

    @pl.when(jnp.logical_not(has_left))
    def _():
        extended[:, pl.ds(0, reach)] = jnp.zeros((2, reach) + extended.shape[2:], BF16)

    @pl.when(jnp.logical_not(has_right))
    def _():
        extended[:, pl.ds(reach + modes, reach)] = jnp.zeros((2, reach) + extended.shape[2:], BF16)

    own_load.wait()

    @pl.when(has_left)
    def _():
        halo_copy(0).wait_recv()

    @pl.when(has_right)
    def _():
        halo_copy(1).wait_recv()

    def couple_mode(m):
        on_liner = liner32[...] == 1
        reach_of = spread32[...]
        for d in range(band):
            inside = jnp.where(on_liner & (reach_of >= abs(d - reach)), 1.0, 0.0).astype(F32)
            for c in range(2):
                raw[pl.ds(c * band + d, 1), :] = coupling32[c, d, pl.ds(m, 1), :] * inside
        weights[...] = jnp.transpose(raw[...])

        @pl.loop(0, points // ROWS)
        def _(b):
            rows = pl.ds(pl.multiple_of(b * ROWS, ROWS), ROWS)
            weight = weights[rows, :]
            real = jnp.zeros((ROWS, extended.shape[3]), F32)
            imag = jnp.zeros((ROWS, extended.shape[3]), F32)
            for d in range(band):
                shifted_r = extended[0, m + d, rows, :].astype(F32)
                shifted_i = extended[1, m + d, rows, :].astype(F32)
                w_r = weight[:, d : d + 1]
                w_i = weight[:, band + d : band + d + 1]
                real = real + w_r * shifted_r - w_i * shifted_i
                imag = imag + w_r * shifted_i + w_i * shifted_r
            result[0, m, rows, :] = real.astype(BF16)
            result[1, m, rows, :] = imag.astype(BF16)

    @pl.loop(0, groups)
    def _(g):
        arrived(0, 0, g)
        for k in range(1, high_count):
            forward_copy(0, k, g).start()
        for k in range(1, high_count):
            arrived(k * 2 - 1, 1, g)
            forward_copy(1, k, g).start()

        @pl.loop(0, step)
        def _(j):
            couple_mode(g * step + j)

    @pl.when(has_right)
    def _():
        halo_copy(0).wait_send()

    @pl.when(has_left)
    def _():
        halo_copy(1).wait_send()

    tiles_load.wait()

    def near_mode(m):
        for r in range(row_tiles):
            total = None
            for slot in range(-1, shards - 1):
                dk, dl = (slot + 1) // 2, (slot + 1) % 2
                source = lax.rem(high + dk, high_count) * 2 + (low if dl == 0 else 1 - low)
                which = index_ref[r, source, m]
                picked = []
                for c in range(2):
                    if slot < 0:
                        block = extended[c, reach + m]
                    else:
                        block = gathered[slot, c, m]
                    chosen = block[:tile]
                    for t in range(1, points // tile):
                        chosen = lax.select(which == t, block[t * tile : (t + 1) * tile], chosen)
                    picked.append(chosen)
                k_r = tiles[m, r, source, 0]
                k_i = tiles[m, r, source, 1]
                left = jnp.concatenate(
                    [jnp.concatenate([k_r, -k_i], axis=1), jnp.concatenate([k_i, k_r], axis=1)], axis=0
                )
                product = jnp.dot(left, jnp.concatenate(picked, axis=0), preferred_element_type=F32)
                total = product if total is None else total + product
            rows = pl.ds(r * tile, tile)
            for c in range(2):
                value = 0.5 * extended[c, reach + m, rows, :].astype(F32)
                value = value + total[c * tile : (c + 1) * tile] + result[c, m, rows, :].astype(F32)
                result[c, m, rows, :] = value.astype(BF16)

    @pl.loop(0, groups)
    def _(g):
        for c in range(2):
            for k in range(high_count):
                own_copy(c, k, g).wait_send()
        arrived(0, 1, g)
        for k in range(1, high_count):
            arrived(k * 2 - 1, 0, g)
            arrived(k * 2, 0, g)
            arrived(k * 2, 1, g)
            for c in range(2):
                forward_copy(c, k, g).wait_send()

        @pl.loop(0, step)
        def _(j):
            near_mode(g * step + j)


def apply_local(mode_devices, shard_count, density, kernel_tiles, tile_index, coupling, spread, liner):
    modes, points, rhs = density.shape[1:]
    band = coupling.shape[1]
    reach = band // 2
    groups = 8 if modes % 8 == 0 else modes
    step = modes // groups
    high_count = shard_count // 2
    dma = pltpu.SemaphoreType.DMA
    hbm = pl.BlockSpec(memory_space=pltpu.HBM)
    vmem = pl.BlockSpec(memory_space=pltpu.VMEM)
    cfg = (shard_count, groups, step, modes, reach, mode_devices)
    return pl.pallas_call(
        functools.partial(operator_kernel, cfg),
        out_shape=pltpu.VMEM(density.shape, BF16),
        in_specs=[
            hbm, hbm, hbm, hbm, hbm, hbm,
        ],
        out_specs=vmem,
        scratch_shapes=[
            pltpu.VMEM((2, modes + 2 * reach, points, rhs), BF16),
            pltpu.VMEM((shard_count - 1, 2, modes, points, rhs), BF16),
            pltpu.VMEM(kernel_tiles.shape, BF16),
            pltpu.VMEM(coupling.shape, BF16),
            pltpu.VMEM((1, points), jnp.int32),
            pltpu.VMEM((1, points), jnp.int32),
            pltpu.SMEM((tile_index.shape[1], tile_index.shape[2], modes), jnp.int32),
            pltpu.VMEM(coupling.shape, F32),
            pltpu.VMEM((128, points), F32),
            pltpu.VMEM((points, 128), F32),
            dma((2, high_count, groups)),
            dma((2, max(high_count - 1, 1), groups)),
            dma((shard_count - 1, 2, groups)),
            dma((2,)),
            dma((2,)),
            dma((6,)),
        ],
        compiler_params=pltpu.CompilerParams(
            collective_id=0, has_side_effects=True, vmem_limit_bytes=56 * MIB
        ),
    )(tile_index.transpose(1, 2, 0), spread.reshape(1, -1), liner.reshape(1, -1), coupling, density, kernel_tiles)


def solution(mesh):
    body = functools.partial(apply_local, mesh.shape["mode"], mesh.shape["blk"])
    return jax.shard_map(
        body,
        mesh=mesh,
        in_specs=(
            P(None, "mode", "blk", None),
            P("mode", "blk", None, None, None, None),
            P("mode", "blk", None),
            P(None, None, "mode", "blk"),
            P("blk"),
            P("blk"),
        ),
        out_specs=P(None, "mode", "blk", None),
        check_vma=False,
    )
```

```python
import functools

import jax
import jax.numpy as jnp
from jax import lax
from jax.experimental import pallas as pl
from jax.experimental.pallas import tpu as pltpu
from jax.sharding import PartitionSpec as P

F32 = jnp.float32
BF16 = jnp.bfloat16
MIB = 1024 * 1024
ROWS = 32


def operator_kernel(
    cfg, index_hbm, spread_ref, liner_ref, coupling_ref, density_ref, tiles_ref, result,
    extended, gathered, tiles, coupling16, spread32, liner32, index_ref, coupling32, raw, weights,
    own_sems, forward_sems, arrive_sems, halo_send, halo_arrive, local_sems,
):
    shards, groups, step, modes, reach, mode_devices = cfg
    high_count = shards // 2
    band = 2 * reach + 1
    row_tiles = tiles_ref.shape[1]
    tile = tiles_ref.shape[-1]
    points = density_ref.shape[2]
    blk = lax.axis_index("blk")
    mode_at = lax.axis_index("mode")
    high, low = blk // 2, blk % 2
    partner = high * 2 + (1 - low)

    def along(k):
        return lax.rem(high + k, high_count) * 2 + low

    def part(g):
        return pl.ds(g * step, step)

    def own_copy(c, k, g):
        target = partner if k == 0 else along(k)
        slot = 0 if k == 0 else (high_count - k) * 2 - 1
        return pltpu.make_async_remote_copy(
            src_ref=density_ref.at[c, part(g)],
            dst_ref=gathered.at[slot, c, part(g)],
            send_sem=own_sems.at[c, k, g],
            recv_sem=arrive_sems.at[slot, c, g],
            device_id={"blk": target},
        )

    def forward_copy(c, k, g):
        if c == 0:
            source, slot, target = 0, (high_count - k) * 2, along(k)
        else:
            source, slot, target = k * 2 - 1, k * 2, partner
        return pltpu.make_async_remote_copy(
            src_ref=gathered.at[source, c, part(g)],
            dst_ref=gathered.at[slot, c, part(g)],
            send_sem=forward_sems.at[c, k - 1, g],
            recv_sem=arrive_sems.at[slot, c, g],
            device_id={"blk": target},
        )

    def arrived(slot, c, g):
        pltpu.make_async_remote_copy(
            src_ref=gathered.at[slot, c, part(g)],
            dst_ref=gathered.at[slot, c, part(g)],
            send_sem=arrive_sems.at[slot, c, g],
            recv_sem=arrive_sems.at[slot, c, g],
            device_id={"blk": partner},
        ).wait_recv()

    def halo_copy(side):
        source = modes - reach if side == 0 else 0
        target = reach + modes if side == 1 else 0
        neighbour = mode_at + 1 if side == 0 else mode_at - 1
        return pltpu.make_async_remote_copy(
            src_ref=density_ref.at[:, pl.ds(source, reach)],
            dst_ref=extended.at[:, pl.ds(target, reach)],
            send_sem=halo_send.at[side],
            recv_sem=halo_arrive.at[side],
            device_id={"mode": neighbour},
        )

    has_left = mode_at > 0
    has_right = mode_at < mode_devices - 1

    own_load = pltpu.make_async_copy(
        density_ref, extended.at[:, pl.ds(reach, modes)], local_sems.at[0]
    )
    tiles_load = pltpu.make_async_copy(tiles_ref, tiles, local_sems.at[1])
    barrier = pltpu.get_barrier_semaphore()
    pl.semaphore_signal(barrier, inc=1, device_id={"blk": partner})
    for k in range(1, high_count):
        pl.semaphore_signal(barrier, inc=1, device_id={"blk": along(k)})

    @pl.when(has_left)
    def _():
        pl.semaphore_signal(barrier, inc=1, device_id={"mode": mode_at - 1})

    @pl.when(has_right)
    def _():
        pl.semaphore_signal(barrier, inc=1, device_id={"mode": mode_at + 1})

    peers = high_count + jnp.where(has_left, 1, 0) + jnp.where(has_right, 1, 0)
    pl.semaphore_wait(barrier, peers)

    @pl.when(has_right)
    def _():
        halo_copy(0).start()

    @pl.when(has_left)
    def _():
        halo_copy(1).start()

    small_loads = [
        pltpu.make_async_copy(source, target, local_sems.at[2 + at])
        for at, (source, target) in enumerate(
            [(coupling_ref, coupling16), (spread_ref, spread32), (liner_ref, liner32), (index_hbm, index_ref)]
        )
    ]
    @pl.loop(0, groups)
    def _(g):
        own_copy(0, 0, g).start()
        for k in range(1, high_count):
            own_copy(1, k, g).start()

    @pl.loop(0, groups)
    def _(g):
        own_copy(1, 0, g).start()
        for k in range(1, high_count):
            own_copy(0, k, g).start()

    for load in small_loads:
        load.start()
    own_load.start()
    tiles_load.start()
    for load in small_loads:
        load.wait()
    coupling32[...] = coupling16[...].astype(F32)
    raw[...] = jnp.zeros_like(raw)

    @pl.when(jnp.logical_not(has_left))
    def _():
        extended[:, pl.ds(0, reach)] = jnp.zeros((2, reach) + extended.shape[2:], BF16)

    @pl.when(jnp.logical_not(has_right))
    def _():
        extended[:, pl.ds(reach + modes, reach)] = jnp.zeros((2, reach) + extended.shape[2:], BF16)

    own_load.wait()

    @pl.when(has_left)
    def _():
        halo_copy(0).wait_recv()

    @pl.when(has_right)
    def _():
        halo_copy(1).wait_recv()

    def couple_mode(m):
        on_liner = liner32[...] == 1
        reach_of = spread32[...]
        for d in range(band):
            inside = jnp.where(on_liner & (reach_of >= abs(d - reach)), 1.0, 0.0).astype(F32)
            for c in range(2):
                raw[pl.ds(c * band + d, 1), :] = coupling32[c, d, pl.ds(m, 1), :] * inside
        weights[...] = jnp.transpose(raw[...])

        @pl.loop(0, points // ROWS)
        def _(b):
            rows = pl.ds(pl.multiple_of(b * ROWS, ROWS), ROWS)
            weight = weights[rows, :]
            real = jnp.zeros((ROWS, extended.shape[3]), F32)
            imag = jnp.zeros((ROWS, extended.shape[3]), F32)
            for d in range(band):
                shifted_r = extended[0, m + d, rows, :].astype(F32)
                shifted_i = extended[1, m + d, rows, :].astype(F32)
                w_r = weight[:, d : d + 1]
                w_i = weight[:, band + d : band + d + 1]
                real = real + w_r * shifted_r - w_i * shifted_i
                imag = imag + w_r * shifted_i + w_i * shifted_r
            result[0, m, rows, :] = real.astype(BF16)
            result[1, m, rows, :] = imag.astype(BF16)

    @pl.loop(0, groups)
    def _(g):
        arrived(0, 0, g)
        for k in range(1, high_count):
            forward_copy(0, k, g).start()
        for k in range(1, high_count):
            arrived(k * 2 - 1, 1, g)
            forward_copy(1, k, g).start()

        @pl.loop(0, step)
        def _(j):
            couple_mode(g * step + j)

    @pl.when(has_right)
    def _():
        halo_copy(0).wait_send()

    @pl.when(has_left)
    def _():
        halo_copy(1).wait_send()

    tiles_load.wait()

    def near_mode(m):
        for r in range(row_tiles):
            total = None
            for slot in range(-1, shards - 1):
                dk, dl = (slot + 1) // 2, (slot + 1) % 2
                source = lax.rem(high + dk, high_count) * 2 + (low if dl == 0 else 1 - low)
                which = index_ref[r, source, m]
                picked = []
                for c in range(2):
                    if slot < 0:
                        block = extended[c, reach + m]
                    else:
                        block = gathered[slot, c, m]
                    chosen = block[:tile]
                    for t in range(1, points // tile):
                        chosen = lax.select(which == t, block[t * tile : (t + 1) * tile], chosen)
                    picked.append(chosen)
                k_r = tiles[m, r, source, 0]
                k_i = tiles[m, r, source, 1]
                left = jnp.concatenate(
                    [jnp.concatenate([k_r, -k_i], axis=1), jnp.concatenate([k_i, k_r], axis=1)], axis=0
                )
                product = jnp.dot(left, jnp.concatenate(picked, axis=0), preferred_element_type=F32)
                total = product if total is None else total + product
            rows = pl.ds(r * tile, tile)
            for c in range(2):
                value = 0.5 * extended[c, reach + m, rows, :].astype(F32)
                value = value + total[c * tile : (c + 1) * tile] + result[c, m, rows, :].astype(F32)
                result[c, m, rows, :] = value.astype(BF16)

    @pl.loop(0, groups)
    def _(g):
        for c in range(2):
            for k in range(high_count):
                own_copy(c, k, g).wait_send()
        arrived(0, 1, g)
        for k in range(1, high_count):
            arrived(k * 2 - 1, 0, g)
            arrived(k * 2, 0, g)
            arrived(k * 2, 1, g)
            for c in range(2):
                forward_copy(c, k, g).wait_send()

        @pl.loop(0, step)
        def _(j):
            near_mode(g * step + j)


def apply_local(mode_devices, shard_count, density, kernel_tiles, tile_index, coupling, spread, liner):
    modes, points, rhs = density.shape[1:]
    band = coupling.shape[1]
    reach = band // 2
    groups = modes
    step = modes // groups
    high_count = shard_count // 2
    dma = pltpu.SemaphoreType.DMA
    hbm = pl.BlockSpec(memory_space=pltpu.HBM)
    vmem = pl.BlockSpec(memory_space=pltpu.VMEM)
    cfg = (shard_count, groups, step, modes, reach, mode_devices)
    return pl.pallas_call(
        functools.partial(operator_kernel, cfg),
        out_shape=pltpu.VMEM(density.shape, BF16),
        in_specs=[
            hbm, hbm, hbm, hbm, hbm, hbm,
        ],
        out_specs=vmem,
        scratch_shapes=[
            pltpu.VMEM((2, modes + 2 * reach, points, rhs), BF16),
            pltpu.VMEM((shard_count - 1, 2, modes, points, rhs), BF16),
            pltpu.VMEM(kernel_tiles.shape, BF16),
            pltpu.VMEM(coupling.shape, BF16),
            pltpu.VMEM((1, points), jnp.int32),
            pltpu.VMEM((1, points), jnp.int32),
            pltpu.SMEM((tile_index.shape[1], tile_index.shape[2], modes), jnp.int32),
            pltpu.VMEM(coupling.shape, F32),
            pltpu.VMEM((128, points), F32),
            pltpu.VMEM((points, 128), F32),
            dma((2, high_count, groups)),
            dma((2, max(high_count - 1, 1), groups)),
            dma((shard_count - 1, 2, groups)),
            dma((2,)),
            dma((2,)),
            dma((6,)),
        ],
        compiler_params=pltpu.CompilerParams(
            collective_id=0, has_side_effects=True, vmem_limit_bytes=56 * MIB
        ),
    )(tile_index.transpose(1, 2, 0), spread.reshape(1, -1), liner.reshape(1, -1), coupling, density, kernel_tiles)


def solution(mesh):
    body = functools.partial(apply_local, mesh.shape["mode"], mesh.shape["blk"])
    return jax.shard_map(
        body,
        mesh=mesh,
        in_specs=(
            P(None, "mode", "blk", None),
            P("mode", "blk", None, None, None, None),
            P("mode", "blk", None),
            P(None, None, "mode", "blk"),
            P("blk"),
            P("blk"),
        ),
        out_specs=P(None, "mode", "blk", None),
        check_vma=False,
    )
```
